256 devices in a mesh: comp: 2 (over core), gx: 16 (over x, z_hi), gy: 8 (over z_lo, y).
Axes of the slice: x: 4, y: 4, z: 8 (z_hi: 4, z_lo: 2; z = z_hi * 2 + z_lo), core: 2. Of those that a mesh axis runs over, the one named last changes fastest.
Arguments:
- final_adjoint: float32 [2, 128, 512, 1024], P('comp', None, 'gx', 'gy'), may hold values from -6 to 6
- innovations: float32 [4, 2, 32768, 128], P(None, 'comp', ('gx', 'gy')), may hold values from -6 to 6
- obs_owner: int32 [4, 2, 32768, 1], P(None, 'comp', ('gx', 'gy')), may hold values from 0 to 127; in each aligned block of 256 rows (0 to 255, 256 to 511, ..., all dimensions but the last counted through in order) at most 4 rows name the same one
- obs_column: int32 [4, 2, 32768], P(None, 'comp', ('gx', 'gy')), may hold values from 0 to 4095
- coupler: int32 [4, 2, 512, 1024], P(None, 'comp', 'gx', 'gy'), may hold values from 0 to 4095
- sea_mask: int32 [512, 1024], P('gx', 'gy'), may hold values 0 or 1
- diffusion: float32 [2, 128], P('comp'), may hold values from 0.02 to 0.24
- vertical: float32 [2, 128, 128], P('comp'), may hold values from -0.5 to 0.5
- flux_out: float32 [2, 5, 128], P('comp'), may hold values from -0.5 to 0.5
- flux_in: float32 [2, 128, 5], P('comp'), may hold values from -1.25 to 1.25
Outputs:
- start_adjoint: float32 [2, 128, 512, 1024], P('comp', None, 'gx', 'gy')
The draws below stay inside these ranges and needn't reach their ends.
Inputs may be any that keep to these rules, and one draw needn't show every extreme that they name: `obs_owner`: among the 256 profiles of one device, one step and one component, no tile is named more than 4 times, a bound that some block reaches.
All inputs are finite; a program needn't handle non-finite values. No bound on the sum of `sea_mask` on one device may be relied on, other than what follows from the above.
Results may differ from the reference program's by a relative error of at most 0.0001.
Values sent between devices are 32-bit elements; how exact they have to be, the bound alone decides.
A program may use at most 64 MiB of HBM per device.

```python
import math
import jax
import jax.numpy as jnp
import numpy as np
from jax import lax

LEV = 128
FLUX = 5
STEPS = 4
CX = 32
CY = 128
OBS_DEV = 256
NX = 512
NY = 1024
NOBS = 32768
CAP = 4
N_GX = 16
N_GY = 8


def plant(result, stream_key, low, high):
    longest = result.shape.index(max(result.shape))
    spots = []
    for shift in (0, 1):
        where = [jax.random.randint(jax.random.fold_in(stream_key, axis), (), 0, length) for axis, length in enumerate(result.shape)]
        where[longest] = (where[longest] + shift) % result.shape[longest]
        spots.append(tuple(where))
    return result.at[spots[0]].set(low).at[spots[1]].set(high)


def block_levels(rng, extent, pieces, low, high):
    loudness = 1.0
    for dim, shards_of in pieces:
        steps = jax.random.uniform(jax.random.fold_in(jax.random.fold_in(rng, 6), dim), (shards_of,), jnp.float32, low / len(pieces), high / len(pieces))
        loudness = loudness * jnp.repeat(jnp.exp(steps), extent[dim] // shards_of).reshape((-1,) + (1,) * (len(extent) - 1 - dim))
    return loudness


def shared_out(key, own, number, rows, count, top, bound, slope):
    sequence = jax.random.permutation(key, count)
    crowded, common = shares(count, rows * top, bound, slope, True), shares(count, rows * top, bound, slope, False)
    places = jnp.arange(count)

    def named(sizes, turn):
        used = int((sizes > 0).sum())
        fixed = max(1, used // 4)
        moved = fixed + (places - fixed + turn * (used - fixed)) % max(1, count - fixed)
        return jnp.zeros((count,), jnp.int32).at[sequence[jnp.where(places < fixed, places, moved)]].set(jnp.asarray(sizes, jnp.int32))

    sizes = jnp.where(number % 4 == 0, named(crowded, number // 4), named(common, number - number // 4 - 1))
    mixed = jax.random.permutation(jax.random.fold_in(own, 3), count)
    donor, receiver = mixed[0:count // 2 * 2:2], mixed[1:count // 2 * 2:2]
    room = jnp.minimum(sizes[donor] - 1, bound - sizes[receiver]) // 2
    room = jnp.where((donor == sequence[0]) | (receiver == sequence[0]) | (sizes[receiver] == 0), 0, jnp.maximum(room, 0))
    moved = jax.random.randint(jax.random.fold_in(own, 4), (count // 2,), 0, 1 << 20) % (room + 1)
    sizes = sizes.at[donor].add(-moved).at[receiver].add(moved)
    items = jnp.searchsorted(jnp.cumsum(sizes), jnp.arange(rows * top), side="right").astype(jnp.int32)
    table = items.reshape(top, rows).T
    table = table[jax.random.permutation(jax.random.fold_in(own, 1), rows)]
    turn = jax.random.randint(jax.random.fold_in(own, 2), (rows, 1), 0, top)
    return jnp.take_along_axis(table, (jnp.arange(top)[None, :] + turn) % top, axis=1)


def shares(amount, total, most, lean, full):
    portions = [(1 << 20) // math.isqrt(rank ** lean) + 1 for rank in range(1, amount + 1)]
    largest = most if full else min(most, max(-(-total // amount), total * portions[0] // sum(portions)))
    least = 1 if total - largest >= amount - 1 else 0
    given, spare = [largest] + [least] * (amount - 1), total - largest - least * (amount - 1)
    while spare > 0:
        free = [i for i in range(1, amount) if given[i] < largest] or [i for i in range(1, amount) if given[i] < most]
        pool, remaining = sum([portions[i] for i in free]), spare
        for i in free:
            more = min(most - given[i], max(1, remaining * portions[i] // pool), spare)
            given[i] = given[i] + more
            spare = spare - more
    return np.array(given)


def bell_draw(rng, extent, width, most, shards=(), held_as=jnp.bfloat16):
    values = width * jax.random.normal(rng, extent, jnp.float32)
    if shards:
        values = values * block_levels(rng, extent, shards, -0.22, 0.18)
    return jnp.clip(values, -most, most).astype(held_as)


def setup_inputs(seed: int = 0) -> dict:
    key_list = jax.random.split(jax.random.key(seed), 11)
    final_adjoint = bell_draw(key_list[0], (2, LEV, NX, NY), 1.0, 6.0, ((0, 2), (2, 16), (3, 8)), jnp.float32)
    innovations = bell_draw(key_list[1], (STEPS, 2, NOBS, LEV), 1.0, 6.0, ((1, 2), (2, 128)), jnp.float32)
    obs_owner_keys = jax.random.split(jax.random.fold_in(key_list[2], 1), STEPS * 2 * NOBS // OBS_DEV)
    obs_owner_turns = jax.random.permutation(jax.random.fold_in(key_list[2], 3), STEPS * 2 * NOBS // OBS_DEV)
    obs_owner = jax.vmap(lambda own, number: shared_out(jax.random.fold_in(key_list[2], 2), own, number, OBS_DEV, N_GX * N_GY, 1, CAP, 2))(obs_owner_keys, obs_owner_turns).reshape((STEPS, 2, NOBS, 1))
    obs_column = plant(jax.random.randint(key_list[3], (STEPS, 2, NOBS), 0, CX * CY), jax.random.fold_in(key_list[3], 1), 0, (CX * CY) - 1).astype(jnp.int32)
    coupler = plant(jax.random.randint(key_list[4], (STEPS, 2, NX, NY), 0, CX * CY), jax.random.fold_in(key_list[4], 1), 0, (CX * CY) - 1).astype(jnp.int32)
    sea_mask = plant((jax.random.randint(key_list[5], (NX, NY), 0, 4) < 3).astype(jnp.int32), jax.random.fold_in(key_list[5], 1), 0, 1)
    diffusion = jnp.clip(jnp.exp(math.log(0.24) - 2.4849066 * jax.random.uniform(key_list[6], (2, LEV), jnp.float32) ** block_levels(key_list[6], (2, LEV), ((0, 2),), -0.2, 0.2)), 0.02, 0.24)
    vertical = bell_draw(key_list[7], (2, LEV, LEV), LEV ** -0.5, 0.5, ((0, 2),), jnp.float32)
    flux_out = bell_draw(key_list[8], (2, FLUX, LEV), LEV ** -0.5, 0.5, ((0, 2),), jnp.float32)
    flux_in = bell_draw(key_list[9], (2, LEV, FLUX), (4 * FLUX) ** -0.5, 1.25, ((0, 2),), jnp.float32)
    return {"final_adjoint": final_adjoint, "innovations": innovations, "obs_owner": obs_owner, "obs_column": obs_column, "coupler": coupler, "sea_mask": sea_mask, "diffusion": diffusion, "vertical": vertical, "flux_out": flux_out, "flux_in": flux_in}


def to_tiles(grid_array):
    field_count = grid_array.shape[0]
    shaped = grid_array.reshape(field_count, N_GX, CX, N_GY, CY).transpose(0, 1, 3, 2, 4)
    return shaped.reshape(field_count, N_GX, N_GY, CX * CY)


def from_tiles(tiled):
    field_count = tiled.shape[0]
    shaped = tiled.reshape(field_count, N_GX, N_GY, CX, CY).transpose(0, 1, 3, 2, 4)
    return shaped.reshape(field_count, NX, NY)


def reference(final_adjoint, innovations, obs_owner, obs_column, coupler, sea_mask, diffusion, vertical, flux_out, flux_in):
    sea_factor = sea_mask.astype(jnp.float32)
    halves = [final_adjoint[0], final_adjoint[1]]
    for step_index in range(STEPS - 1, -1, -1):
        surfaces = []
        for half_index in range(2):
            column_state = halves[half_index]
            owners = obs_owner[step_index, half_index, :, 0]
            columns = obs_column[step_index, half_index]
            obs_rows = (owners // N_GY) * CX + columns // CY
            obs_cols = (owners % N_GY) * CY + columns % CY
            column_state = column_state.at[:, obs_rows, obs_cols].add(innovations[step_index, half_index].T)
            padded = jnp.pad(column_state, ((0, 0), (1, 1), (1, 1)))
            beside = padded[:, 2:, 1:-1] + padded[:, :-2, 1:-1] + padded[:, 1:-1, 2:] + padded[:, 1:-1, :-2]
            column_state = column_state + diffusion[half_index][:, None, None] * (beside - 4.0 * column_state)
            column_state = jnp.einsum('kl,kxy->lxy', vertical[half_index], column_state, precision=lax.Precision.HIGHEST)
            if half_index == 0:
                column_state = column_state * sea_factor
            halves[half_index] = column_state
            surfaces.append(jnp.einsum('fl,lxy->fxy', flux_out[half_index], column_state, precision=lax.Precision.HIGHEST))
        for half_index in range(2):
            partner = to_tiles(surfaces[1 - half_index])
            indices = to_tiles(coupler[step_index, half_index][None])
            received = from_tiles(jnp.take_along_axis(partner, jnp.broadcast_to(indices, partner.shape), axis=3))
            halves[half_index] = halves[half_index] + jnp.einsum('lf,fxy->lxy', flux_in[half_index], received, precision=lax.Precision.HIGHEST)
    return jnp.stack(halves)
```

```python
import jax
import jax.numpy as jnp
from jax import lax
from jax.experimental import pallas as pl
from jax.experimental.pallas import tpu as pltpu
from jax.sharding import PartitionSpec as P

MESH = pl.DeviceIdType.MESH
STEPS = 4
ROWS = 32
COLS = 128
LEV = 128
PROF = 256
SLOTS = 512
FIELDS = 5
HALF = ROWS // 2
BF = jnp.bfloat16
F32 = jnp.float32
I32 = jnp.int32

NN = (((1,), (0,)), ((), ()))
NT = (((1,), (1,)), ((), ()))
TN = (((0,), (0,)), ((), ()))


def dot(a, b, dims):
    return lax.dot_general(a, b, dims, preferred_element_type=F32)


def halves(value):
    high = value.astype(BF)
    low = (value - high.astype(F32)).astype(BF)
    return high, low


def at_chip(x, y, z):
    return {"gx": x * 4 + z // 2, "gy": lax.rem(z, 2) * 4 + y}


def kernel(
    state_hbm,
    innov_hbm,
    owner_ref,
    column_ref,
    coupler_ref,
    mask_ref,
    diff_ref,
    vert_ref,
    fout_ref,
    fin_ref,
    out_hbm,
    grid_in,
    innov,
    ext,
    send_buf,
    mid_buf,
    prof_buf,
    state_hl,
    mask_full,
    onehot,
    prof_hl,
    col_send,
    col_mid,
    col_line,
    col_recv,
    col_wide,
    col_rows,
    surf,
    partner,
    received,
    weights,
    weights_t,
    surf_w,
    fin_w,
    fin_wt,
    small,
    load_sem,
    s1,
    r1,
    l1,
    s2,
    r2,
    l2,
    col_sem,
    halo_s,
    halo_r,
    part_s,
    part_r,
    out_sem,
):
    comp = lax.axis_index("comp")
    gx = lax.axis_index("gx")
    gy = lax.axis_index("gy")
    x, y = gx // 4, lax.rem(gy, 4)
    z = lax.rem(gx, 4) * 2 + gy // 4
    q = x * 4 + y

    load_innov = pltpu.make_async_copy(innov_hbm, innov, load_sem.at[0])
    load_state = pltpu.make_async_copy(state_hbm, grid_in, load_sem.at[1])
    load_innov.start()
    load_state.start()

    def zero_edges(step, carry):
        ext[step, 0] = jnp.zeros((144, LEV), F32)
        ext[step, ROWS + 1] = jnp.zeros((144, LEV), F32)
        ext[step, 1 : ROWS + 1, 0:8, :] = jnp.zeros((ROWS, 8, LEV), F32)
        ext[step, 1 : ROWS + 1, 136:144, :] = jnp.zeros((ROWS, 8, LEV), F32)
        return carry

    lax.fori_loop(0, STEPS, zero_edges, 0)

    def xy_peer(i):
        return lax.rem(x + i // 4, 4), lax.rem(y + lax.rem(i, 4), 4)

    barrier = pltpu.get_barrier_semaphore()

    def greet(target):
        pl.semaphore_signal(barrier, inc=1, device_id=target, device_id_type=MESH)

    for i in range(1, 16):
        x2, y2 = xy_peer(jnp.int32(i))
        greet(at_chip(x2, y2, z))
    for i in range(1, 8):
        greet(at_chip(x, y, lax.rem(z + i, 8)))
    greet({"comp": 1 - comp})

    sides = (
        (gx > 0, {"gx": gx - 1}),
        (gx < 15, {"gx": gx + 1}),
        (gy > 0, {"gy": gy - 1}),
        (gy < 7, {"gy": gy + 1}),
    )
    for there, target in sides:

        @pl.when(there)
        def _(target=target):
            greet(target)

    greeted = 23
    for there, _ in sides:
        greeted = greeted + jnp.where(there, 1, 0)

    vert = vert_ref[...]
    v_high, v_low = halves(vert)
    weights[0:128, 0:128] = v_high
    weights[128:256, 0:128] = v_high
    weights[0:128, 128:256] = v_low
    weights[128:256, 128:256] = v_low
    vt_high, vt_low = halves(vert.T)
    weights_t[0:128, 0:128] = vt_high
    weights_t[0:128, 128:256] = vt_high
    weights_t[128:256, 0:128] = vt_low
    weights_t[128:256, 128:256] = vt_low
    small[...] = jnp.zeros((16, LEV), F32)
    small[0:FIELDS, :] = fout_ref[...]
    small[8 : 8 + FIELDS, :] = fin_ref[...]
    flux_w = lax.dot_general(
        small[0:8, :], vert, NT, precision=lax.Precision.HIGHEST, preferred_element_type=F32
    )
    g_high = flux_w.astype(BF).astype(F32)
    g_both = jnp.concatenate([g_high, flux_w - g_high], axis=0).astype(BF)
    surf_w[:, 0:128] = g_both
    surf_w[:, 128:256] = g_both
    fin = small[8:16, :]
    f_high = fin.astype(BF).astype(F32)
    f_all = jnp.concatenate([f_high, f_high, fin - f_high, jnp.zeros((8, LEV), F32)], axis=0)
    fin_w[...] = f_all.astype(BF)
    f_pad = jnp.concatenate([f_all, jnp.zeros((96, LEV), F32)], axis=0)
    fin_wt[...] = f_pad.T.astype(BF)
    received[...] = jnp.zeros((ROWS, 8, COLS), F32)

    lane_b = lax.broadcasted_iota(I32, (128, 128), 1)
    sub_b = lax.broadcasted_iota(I32, (128, 128), 0)
    earlier = sub_b < lane_b

    def slot_of(step):
        owner = owner_ref[pl.ds(step, 1), :]
        first, second = owner[:, 0:128], owner[:, 128:256]
        first_b = jnp.broadcast_to(first, (128, 128))
        second_b = jnp.broadcast_to(second, (128, 128))
        first_t = first_b.astype(F32).T.astype(I32)
        second_t = second_b.astype(F32).T.astype(I32)
        one = jnp.where((first_t == first_b) & earlier, 1, 0)
        two = jnp.where(first_t == second_b, 1, 0)
        three = jnp.where((second_t == second_b) & earlier, 1, 0)
        rank = jnp.concatenate(
            [
                jnp.sum(one, axis=0, keepdims=True),
                jnp.sum(two + three, axis=0, keepdims=True),
            ],
            axis=1,
        )
        owner_q = (owner >> 5) * 4 + (owner & 3)
        owner_z = ((owner >> 3) & 3) * 2 + ((owner >> 2) & 1)
        return owner_q, owner_z, rank

    def pack(step):
        owner_q, owner_z, rank = slot_of(step)
        slot = (owner_q * 8 + owner_z) * 4 + rank
        placing = jnp.where(
            jnp.broadcast_to(slot, (SLOTS, PROF)) == lax.broadcasted_iota(I32, (SLOTS, PROF), 0),
            1.0,
            0.0,
        ).astype(BF)
        high, low = halves(innov[step])
        placed = dot(placing, jnp.concatenate([high, low], axis=1), NN)
        send_buf[step] = (placed[:, 0:LEV] + placed[:, LEV:]).reshape(16, 32, LEV)
        columns = column_ref[pl.ds(step, 1), :]
        to_q = jnp.broadcast_to(owner_q, (16, PROF)) == lax.broadcasted_iota(I32, (16, PROF), 0)
        row_part = jnp.where(to_q, (columns >> 7).astype(F32), 0.0)
        col_part = jnp.where(to_q, (columns & 127).astype(F32), 0.0)
        both = jnp.concatenate([row_part, col_part], axis=0).astype(BF)
        lane = owner_z * 16 + step * 4 + rank
        spread = jnp.where(
            jnp.broadcast_to(lane, (128, PROF)) == lax.broadcasted_iota(I32, (128, PROF), 0),
            1.0,
            0.0,
        ).astype(BF)
        lines = dot(both, spread, NT)
        return lines[0:16] * 128.0 + lines[16:32]

    def first_leg(step):
        pltpu.make_async_copy(send_buf.at[step, q], mid_buf.at[step, q], l1.at[step]).start()

        def send(i, carry):
            x2, y2 = xy_peer(i)
            pltpu.make_async_remote_copy(
                send_buf.at[step, x2 * 4 + y2],
                mid_buf.at[step, q],
                s1.at[step],
                r1.at[step],
                device_id=at_chip(x2, y2, z),
                device_id_type=MESH,
            ).start()
            return carry

        lax.fori_loop(1, 16, send, 0)

    def many(ref, sem):
        return pltpu.make_async_copy(ref, ref, sem)

    def second_leg(step):
        pltpu.make_async_copy(send_buf.at[step, q], mid_buf.at[step, q], l1.at[step]).wait()
        many(mid_buf.at[step, pl.ds(0, 15)], r1.at[step]).wait()

        def block(z2):
            return mid_buf.at[step, :, pl.ds(pl.multiple_of(z2 * 4, 4), 4), :]

        pltpu.make_async_copy(block(z), prof_buf.at[step, z], l2.at[step]).start()

        def send(i, carry):
            z2 = lax.rem(z + i, 8)
            pltpu.make_async_remote_copy(
                block(z2),
                prof_buf.at[step, z],
                s2.at[step],
                r2.at[step],
                device_id=at_chip(x, y, z2),
                device_id_type=MESH,
            ).start()
            return carry

        lax.fori_loop(1, 8, send, 0)

    def arrived(step):
        pltpu.make_async_copy(
            mid_buf.at[step, :, pl.ds(0, 4), :], prof_buf.at[step, z], l2.at[step]
        ).wait()
        many(prof_buf.at[step, pl.ds(0, 7)], r2.at[step]).wait()

    load_innov.wait()
    lines = pack(3)
    pl.semaphore_wait(barrier, greeted)
    first_leg(3)
    for step in (2, 1, 0):
        lines = lines + pack(step)
        first_leg(step)
    col_send[...] = jnp.broadcast_to(lines[:, None, :], (16, 8, LEV))
    col_mid[pl.ds(q, 1)] = col_send[pl.ds(q, 1)]

    def send_columns(i, carry):
        x2, y2 = xy_peer(i)
        pltpu.make_async_remote_copy(
            col_send.at[x2 * 4 + y2],
            col_mid.at[q],
            col_sem.at[0],
            col_sem.at[1],
            device_id=at_chip(x2, y2, z),
            device_id_type=MESH,
        ).start()
        return carry

    lax.fori_loop(1, 16, send_columns, 0)
    second_leg(3)

    load_state.wait()

    def turn(i, carry):
        for u in range(4):
            r = i * 4 + u
            ext[3, r + 1, 8:136, :] = grid_in[pl.ds(r, LEV, stride=ROWS), :].T
        return carry

    lax.fori_loop(0, ROWS // 4, turn, 0)

    many(col_mid.at[pl.ds(0, 15)], col_sem.at[1]).wait()
    col_line[...] = col_mid[:, 0, :]
    col_recv[pl.ds(z, 1)] = col_line[...][None]

    def send_lines(i, carry):
        z2 = lax.rem(z + i, 8)
        pltpu.make_async_remote_copy(
            col_line,
            col_recv.at[z],
            col_sem.at[2],
            col_sem.at[3],
            device_id=at_chip(x, y, z2),
            device_id_type=MESH,
        ).start()
        return carry

    lax.fori_loop(1, 8, send_lines, 0)
    second_leg(2)

    is_ocean = comp == 0

    def spread_mask(i, carry):
        for u in range(4):
            r = i * 4 + u
            line = jnp.where(is_ocean, mask_ref[pl.ds(r, 1), :].astype(F32), 1.0)
            mask_full[r] = jnp.broadcast_to(line, (COLS, COLS)).T
        return carry

    lax.fori_loop(0, ROWS // 4, spread_mask, 0)

    many(col_recv.at[pl.ds(0, 7)], col_sem.at[3]).wait()
    came = col_recv[...].reshape(128, 128)
    came_row = jnp.floor(came * (1.0 / 128.0))
    came_col = came - came_row * 128.0
    source = lax.broadcasted_iota(I32, (128, SLOTS), 0)
    repeat = jnp.where(source == (lax.broadcasted_iota(I32, (128, SLOTS), 1) >> 2), 1.0, 0.0).astype(BF)
    own_slot = (lax.broadcasted_iota(I32, (16, SLOTS), 0) & 3) == (
        lax.broadcasted_iota(I32, (16, SLOTS), 1) & 3
    )
    for part, value in enumerate((came_row, came_col)):
        col_wide[...] = dot(value.astype(BF), repeat, TN)
        mine = col_wide[pl.ds(pl.multiple_of(z * 16, 16), 16), :]
        mine = jnp.where(own_slot, mine, 0.0)
        for step in range(STEPS):
            col_rows[part, step : step + 1, :] = jnp.sum(
                mine[step * 4 : step * 4 + 4], axis=0, keepdims=True
            )

    def chunk_rows(i):
        return pl.ds(1 + i * HALF, HALF)

    def scatter(step):
        high, low = halves(prof_buf[step].reshape(SLOTS, LEV))
        prof_hl[:, 0:LEV] = high
        prof_hl[:, LEV:] = low
        rows_id = col_rows[0, step : step + 1, :]
        cols_id = col_rows[1, step : step + 1, :]
        cell = lax.broadcasted_iota(I32, (COLS, SLOTS), 0).astype(F32).astype(BF)

        def chunk(i, carry):
            for u in range(HALF):
                r = (i * HALF + u).astype(F32)
                wanted = jnp.where(rows_id == r, cols_id, -1.0)
                wanted = jnp.broadcast_to(wanted, (16, SLOTS)).astype(BF)
                wanted = jnp.concatenate([wanted] * 8, axis=0)
                onehot[u * COLS : (u + 1) * COLS, :] = jnp.where(wanted == cell, BF(1), BF(0))
            added = dot(onehot[...], prof_hl[...], NN)
            added = (added[:, 0:LEV] + added[:, LEV:]).reshape(HALF, COLS, LEV)
            ext[step, chunk_rows(i), 8:136, :] = ext[step, chunk_rows(i), 8:136, :] + added
            return carry

        lax.fori_loop(0, 2, chunk, 0)

    def halo_copy(step, side):
        row, col = pl.ds(8, COLS), pl.ds(1, ROWS)
        src, dst = (
            (ext.at[step, 1, row], ext.at[step, ROWS + 1, row]),
            (ext.at[step, ROWS, row], ext.at[step, 0, row]),
            (ext.at[step, col, pl.ds(8, 1)], ext.at[step, col, pl.ds(136, 1)]),
            (ext.at[step, col, pl.ds(135, 1)], ext.at[step, col, pl.ds(7, 1)]),
        )[side]
        return pltpu.make_async_remote_copy(
            src,
            dst,
            halo_s.at[step, side],
            halo_r.at[step, side],
            device_id=sides[side][1],
            device_id_type=MESH,
        )

    def halo_start(step):
        for side in range(4):

            @pl.when(sides[side][0])
            def _(side=side):
                halo_copy(step, side).start()

    def halo_wait(step):
        for side in range(4):

            @pl.when(sides[side][0])
            def _(side=side):
                halo_copy(step, side).wait_send()
                halo_copy(step, side ^ 1).wait_recv()

    def stencil(step):
        rate = diff_ref[0:1, :]
        rest = 1.0 - 4.0 * rate

        def rows(i, carry):
            for u in range(4):
                r = i * 4 + u
                here = ext[step, r + 1, 8:136, :]
                beside = (
                    ext[step, r, 8:136, :]
                    + ext[step, r + 2, 8:136, :]
                    + ext[step, r + 1, 7:135, :]
                    + ext[step, r + 1, 9:137, :]
                )
                value = (here * rest + beside * rate) * mask_full[r]
                high, low = halves(value)
                at = pl.ds(pl.multiple_of(r * COLS, COLS), COLS)
                state_hl[at, 0:LEV] = high
                state_hl[at, LEV:] = low
            return carry

        lax.fori_loop(0, ROWS // 4, rows, 0)

    def chunk_cells(i):
        return pl.ds(pl.multiple_of(i * HALF * COLS, HALF * COLS), HALF * COLS)

    def surfaces(step):
        def chunk(i, carry):
            both = dot(surf_w[...], state_hl[chunk_cells(i), :], NT)
            total = both[0:8] + both[8:16]
            for j in range(HALF):
                surf[step, i * HALF + j] = total[:, j * COLS : (j + 1) * COLS]
            return carry

        lax.fori_loop(0, 2, chunk, 0)

    def partner_copy(step):
        return pltpu.make_async_remote_copy(
            surf.at[step],
            partner.at[step],
            part_s.at[step],
            part_r.at[step],
            device_id={"comp": 1 - comp},
            device_id_type=MESH,
        )

    def vertical(step):
        def chunk(i, carry):
            mixed = dot(state_hl[chunk_cells(i), :], weights[...], NN)
            mixed = mixed[:, 0:LEV] + mixed[:, LEV:]
            ext[step, chunk_rows(i), 8:136, :] = mixed.reshape(HALF, COLS, LEV)
            return carry

        lax.fori_loop(0, 2, chunk, 0)

    def couple(step):
        def block(b, carry):
            index = coupler_ref[step, pl.ds(pl.multiple_of(b * 8, 8), 8), :]
            lane, row = index & 127, index >> 7
            sums = [jnp.zeros((8, COLS), F32) for _ in range(FIELDS)]
            for r in range(ROWS):
                hit = row == r
                for f in range(FIELDS):
                    line = jnp.broadcast_to(partner[step, r, f : f + 1, :], (8, COLS))
                    sums[f] = jnp.where(hit, jnp.take_along_axis(line, lane, axis=1), sums[f])
            for f in range(FIELDS):
                for j in range(8):
                    received[b * 8 + j, f : f + 1, :] = sums[f][j : j + 1, :]
            return carry

        lax.fori_loop(0, 4, block, 0)

    def received_parts(i):
        value = jnp.concatenate([received[i * HALF + j] for j in range(HALF)], axis=1)
        high = value.astype(BF).astype(F32)
        low = value - high
        return jnp.concatenate([high, low, high, low], axis=0).astype(BF)

    def add_fluxes(step):
        def chunk(i, carry):
            added = dot(received_parts(i), fin_w[...], TN).reshape(HALF, COLS, LEV)
            ext[step, chunk_rows(i), 8:136, :] = ext[step, chunk_rows(i), 8:136, :] + added
            return carry

        lax.fori_loop(0, 2, chunk, 0)

    def finish():
        def chunk(i, carry):
            mixed = dot(weights_t[...], state_hl[chunk_cells(i), :], NT)
            mixed = mixed[0:LEV] + mixed[LEV:]
            mixed = mixed + dot(fin_wt[:, 0:32], received_parts(i), NN)
            for j in range(HALF):
                grid_in[pl.ds(i * HALF + j, LEV, stride=ROWS), :] = mixed[
                    :, j * COLS : (j + 1) * COLS
                ]
            return carry

        lax.fori_loop(0, 2, chunk, 0)

    for step in (3, 2, 1, 0):
        if step < 3:
            vertical(step)
        if step == 3:
            second_leg(1)
        arrived(step)
        scatter(step)
        if step < 3:
            partner_copy(step + 1).wait()
            couple(step + 1)
            add_fluxes(step)
        halo_start(step)
        if step == 3:
            second_leg(0)
        halo_wait(step)
        stencil(step)
        surfaces(step)
        partner_copy(step).start()
    partner_copy(0).wait()
    couple(0)
    finish()
    store = pltpu.make_async_copy(grid_in, out_hbm, out_sem)
    store.start()

    many(col_mid.at[pl.ds(0, 15)], col_sem.at[0]).wait()
    many(col_recv.at[pl.ds(0, 7)], col_sem.at[2]).wait()
    for step in range(STEPS):
        many(mid_buf.at[step, pl.ds(0, 15)], s1.at[step]).wait()
        many(prof_buf.at[step, pl.ds(0, 7)], s2.at[step]).wait()
    store.wait()


def body(
    final_adjoint,
    innovations,
    obs_owner,
    obs_column,
    coupler,
    sea_mask,
    diffusion,
    vertical,
    flux_out,
    flux_in,
):
    whole = pl.BlockSpec(memory_space=pl.ANY)
    near = pl.BlockSpec(memory_space=pltpu.VMEM)
    dma = pltpu.SemaphoreType.DMA
    result = pl.pallas_call(
        kernel,
        out_shape=jax.ShapeDtypeStruct((LEV * ROWS, COLS), F32),
        in_specs=[whole, whole] + [near] * 8,
        out_specs=whole,
        scratch_shapes=[
            pltpu.VMEM((LEV * ROWS, COLS), F32),
            pltpu.VMEM((STEPS, PROF, LEV), F32),
            pltpu.VMEM((STEPS, ROWS + 2, 144, LEV), F32),
            pltpu.VMEM((STEPS, 16, 32, LEV), F32),
            pltpu.VMEM((STEPS, 16, 32, LEV), F32),
            pltpu.VMEM((STEPS, 8, 16, 4, LEV), F32),
            pltpu.VMEM((ROWS * COLS, 2 * LEV), BF),
            pltpu.VMEM((ROWS, COLS, LEV), F32),
            pltpu.VMEM((HALF * COLS, SLOTS), BF),
            pltpu.VMEM((SLOTS, 2 * LEV), BF),
            pltpu.VMEM((16, 8, LEV), F32),
            pltpu.VMEM((16, 8, LEV), F32),
            pltpu.VMEM((16, LEV), F32),
            pltpu.VMEM((8, 16, LEV), F32),
            pltpu.VMEM((128, SLOTS), F32),
            pltpu.VMEM((2, STEPS, SLOTS), F32),
            pltpu.VMEM((STEPS, ROWS, 8, COLS), F32),
            pltpu.VMEM((STEPS, ROWS, 8, COLS), F32),
            pltpu.VMEM((ROWS, 8, COLS), F32),
            pltpu.VMEM((256, 256), BF),
            pltpu.VMEM((256, 256), BF),
            pltpu.VMEM((16, 256), BF),
            pltpu.VMEM((32, LEV), BF),
            pltpu.VMEM((LEV, 128), BF),
            pltpu.VMEM((16, LEV), F32),
            dma((2,)),
            dma((STEPS,)),
            dma((STEPS,)),
            dma((STEPS,)),
            dma((STEPS,)),
            dma((STEPS,)),
            dma((STEPS,)),
            dma((4,)),
            dma((STEPS, 4)),
            dma((STEPS, 4)),
            dma((STEPS,)),
            dma((STEPS,)),
            dma,
        ],
        compiler_params=pltpu.CompilerParams(
            collective_id=0, has_side_effects=True, vmem_limit_bytes=52 * 2**20
        ),
    )(
        final_adjoint.reshape(LEV * ROWS, COLS),
        innovations.reshape(STEPS, PROF, LEV),
        obs_owner.reshape(STEPS, PROF),
        obs_column.reshape(STEPS, PROF),
        coupler.reshape(STEPS, ROWS, COLS),
        sea_mask,
        diffusion,
        vertical[0],
        flux_out[0],
        flux_in[0].T,
    )
    return result.reshape(1, LEV, ROWS, COLS)


def solution(mesh):
    placed = (
        P("comp", None, "gx", "gy"),
        P(None, "comp", ("gx", "gy"), None),
        P(None, "comp", ("gx", "gy"), None),
        P(None, "comp", ("gx", "gy")),
        P(None, "comp", "gx", "gy"),
        P("gx", "gy"),
        P("comp", None),
        P("comp", None, None),
        P("comp", None, None),
        P("comp", None, None),
    )
    return jax.shard_map(
        body, mesh=mesh, in_specs=placed, out_specs=P("comp", None, "gx", "gy"), check_vma=False
    )
```

```python
import jax
import jax.numpy as jnp
from jax import lax
from jax.experimental import pallas as pl
from jax.experimental.pallas import tpu as pltpu
from jax.sharding import PartitionSpec as P

MESH = pl.DeviceIdType.MESH
STEPS = 4
ROWS = 32
COLS = 128
LEV = 128
PROF = 256
SLOTS = 512
FIELDS = 5
HALF = ROWS // 2
BF = jnp.bfloat16
F32 = jnp.float32
I32 = jnp.int32

NN = (((1,), (0,)), ((), ()))
NT = (((1,), (1,)), ((), ()))
TN = (((0,), (0,)), ((), ()))


def dot(a, b, dims):
    return lax.dot_general(a, b, dims, preferred_element_type=F32)


def halves(value):
    high = value.astype(BF)
    low = (value - high.astype(F32)).astype(BF)
    return high, low


def at_chip(x, y, z):
    return {"gx": x * 4 + z // 2, "gy": lax.rem(z, 2) * 4 + y}


def kernel(
    state_hbm,
    innov_hbm,
    owner_hbm,
    column_hbm,
    coupler_hbm,
    mask_hbm,
    diff_hbm,
    vert_hbm,
    fout_hbm,
    fin_hbm,
    out_hbm,
    owner_ref,
    column_ref,
    coupler_ref,
    mask_ref,
    diff_ref,
    vert_ref,
    fout_ref,
    fin_ref,
    grid_in,
    innov,
    ext,
    send_buf,
    mid_buf,
    prof_buf,
    state_hl,
    mask_full,
    onehot,
    prof_hl,
    col_send,
    col_mid,
    col_line,
    col_recv,
    col_wide,
    col_rows,
    surf,
    partner,
    received,
    weights,
    weights_t,
    surf_w,
    fin_w,
    fin_wt,
    small,
    edge_row,
    edge_col,
    halo_col,
    edge_flux,
    halo_flux,
    load_sem,
    s1,
    r1,
    l1,
    s2,
    r2,
    l2,
    col_sem,
    halo_s,
    halo_r,
    part_s,
    part_r,
    out_sem,
):
    comp = lax.axis_index("comp")
    gx = lax.axis_index("gx")
    gy = lax.axis_index("gy")
    x, y = gx // 4, lax.rem(gy, 4)
    z = lax.rem(gx, 4) * 2 + gy // 4
    q = x * 4 + y

    loads = [
        pltpu.make_async_copy(src, dst, load_sem.at[i])
        for i, (src, dst) in enumerate(
            (
                (owner_hbm, owner_ref),
                (innov_hbm, innov),
                (vert_hbm, vert_ref),
                (fout_hbm, fout_ref),
                (fin_hbm, fin_ref),
                (column_hbm, column_ref),
                (coupler_hbm, coupler_ref),
                (mask_hbm, mask_ref),
                (diff_hbm, diff_ref),
            )
        )
    ]
    for load in loads:
        load.start()

    def load_row(r, carry):
        pltpu.make_async_copy(state_hbm.at[:, r, :], grid_in.at[r], out_sem).start()
        return carry

    lax.fori_loop(0, ROWS, load_row, 0)

    def zero_edges(step, carry):
        ext[step, 0] = jnp.zeros((144, LEV), F32)
        ext[step, ROWS + 1] = jnp.zeros((144, LEV), F32)
        halo_col[step] = jnp.zeros((2, ROWS, LEV), F32)
        halo_flux[step] = jnp.zeros((2, 8, COLS), F32)
        return carry

    lax.fori_loop(0, STEPS, zero_edges, 0)

    def xy_peer(i):
        return lax.rem(x + i // 4, 4), lax.rem(y + lax.rem(i, 4), 4)

    barrier = pltpu.get_barrier_semaphore()

    def greet(target):
        pl.semaphore_signal(barrier, inc=1, device_id=target, device_id_type=MESH)

    for i in range(1, 16):
        x2, y2 = xy_peer(jnp.int32(i))
        greet(at_chip(x2, y2, z))
    for i in range(1, 8):
        greet(at_chip(x, y, lax.rem(z + i, 8)))
    greet({"comp": 1 - comp})

    sides = (
        (gx > 0, {"gx": gx - 1}),
        (gx < 15, {"gx": gx + 1}),
        (gy > 0, {"gy": gy - 1}),
        (gy < 7, {"gy": gy + 1}),
    )
    for there, target in sides:

        @pl.when(there)
        def _(target=target):
            greet(target)

    greeted = 23
    for there, _ in sides:
        greeted = greeted + jnp.where(there, 1, 0)

    for load in loads[2:5]:
        load.wait()
    vert = vert_ref[...]
    v_high, v_low = halves(vert)
    weights[0:128, 0:128] = v_high
    weights[128:256, 0:128] = v_high
    weights[0:128, 128:256] = v_low
    weights[128:256, 128:256] = v_low
    vt_high, vt_low = halves(vert.T)
    weights_t[0:128, 0:128] = vt_high
    weights_t[0:128, 128:256] = vt_high
    weights_t[128:256, 0:128] = vt_low
    weights_t[128:256, 128:256] = vt_low
    small[...] = jnp.zeros((16, LEV), F32)
    for f in range(FIELDS):
        small[f : f + 1, :] = fout_ref[f]
        small[8 + f : 9 + f, :] = fin_ref[f]
    flux_w = lax.dot_general(
        small[0:8, :], vert, NT, precision=lax.Precision.HIGHEST, preferred_element_type=F32
    )
    g_high = flux_w.astype(BF).astype(F32)
    g_both = jnp.concatenate([g_high, flux_w - g_high], axis=0).astype(BF)
    surf_w[:, 0:128] = g_both
    surf_w[:, 128:256] = g_both
    fin = small[8:16, :]
    f_high = fin.astype(BF).astype(F32)
    f_all = jnp.concatenate([f_high, f_high, fin - f_high, jnp.zeros((8, LEV), F32)], axis=0)
    fin_w[...] = f_all.astype(BF)
    f_pad = jnp.concatenate([f_all, jnp.zeros((96, LEV), F32)], axis=0)
    fin_wt[...] = f_pad.T.astype(BF)
    received[...] = jnp.zeros((ROWS, 8, COLS), F32)

    lane_b = lax.broadcasted_iota(I32, (128, 128), 1)
    sub_b = lax.broadcasted_iota(I32, (128, 128), 0)
    earlier = sub_b < lane_b

    def slot_of(step):
        owner = owner_ref[step]
        first, second = owner[:, 0:128], owner[:, 128:256]
        first_b = jnp.broadcast_to(first, (128, 128))
        second_b = jnp.broadcast_to(second, (128, 128))
        first_t = first_b.astype(F32).T.astype(I32)
        second_t = second_b.astype(F32).T.astype(I32)
        one = jnp.where((first_t == first_b) & earlier, 1, 0)
        two = jnp.where(first_t == second_b, 1, 0)
        three = jnp.where((second_t == second_b) & earlier, 1, 0)
        rank = jnp.concatenate(
            [
                jnp.sum(one, axis=0, keepdims=True),
                jnp.sum(two + three, axis=0, keepdims=True),
            ],
            axis=1,
        )
        owner_q = (owner >> 5) * 4 + (owner & 3)
        owner_z = ((owner >> 3) & 3) * 2 + ((owner >> 2) & 1)
        return owner_q, owner_z, rank

    def pack(step):
        owner_q, owner_z, rank = slot_of(step)
        slot = (owner_q * 8 + owner_z) * 4 + rank
        placing = jnp.where(
            jnp.broadcast_to(slot, (SLOTS, PROF)) == lax.broadcasted_iota(I32, (SLOTS, PROF), 0),
            1.0,
            0.0,
        ).astype(BF)
        high, low = halves(innov[step])
        placed = dot(placing, jnp.concatenate([high, low], axis=1), NN)
        send_buf[step] = (placed[:, 0:LEV] + placed[:, LEV:]).reshape(16, 32, LEV)
        columns = column_ref[step]
        to_q = jnp.broadcast_to(owner_q, (16, PROF)) == lax.broadcasted_iota(I32, (16, PROF), 0)
        row_part = jnp.where(to_q, (columns >> 7).astype(F32), 0.0)
        col_part = jnp.where(to_q, (columns & 127).astype(F32), 0.0)
        both = jnp.concatenate([row_part, col_part], axis=0).astype(BF)
        lane = owner_z * 16 + step * 4 + rank
        spread = jnp.where(
            jnp.broadcast_to(lane, (128, PROF)) == lax.broadcasted_iota(I32, (128, PROF), 0),
            1.0,
            0.0,
        ).astype(BF)
        lines = dot(both, spread, NT)
        return lines[0:16] * 128.0 + lines[16:32]

    def first_leg(step):
        pltpu.make_async_copy(send_buf.at[step, q], mid_buf.at[step, q], l1.at[step]).start()

        def send(i, carry):
            x2, y2 = xy_peer(i)
            pltpu.make_async_remote_copy(
                send_buf.at[step, x2 * 4 + y2],
                mid_buf.at[step, q],
                s1.at[step],
                r1.at[step],
                device_id=at_chip(x2, y2, z),
                device_id_type=MESH,
            ).start()
            return carry

        lax.fori_loop(1, 16, send, 0)

    def many(ref, sem):
        return pltpu.make_async_copy(ref, ref, sem)

    def second_leg(step):
        pltpu.make_async_copy(send_buf.at[step, q], mid_buf.at[step, q], l1.at[step]).wait()
        many(mid_buf.at[step, pl.ds(0, 15)], r1.at[step]).wait()

        def block(z2):
            return mid_buf.at[step, :, pl.ds(pl.multiple_of(z2 * 4, 4), 4), :]

        pltpu.make_async_copy(block(z), prof_buf.at[step, z], l2.at[step]).start()

        def send(i, carry):
            z2 = lax.rem(z + i, 8)
            pltpu.make_async_remote_copy(
                block(z2),
                prof_buf.at[step, z],
                s2.at[step],
                r2.at[step],
                device_id=at_chip(x, y, z2),
                device_id_type=MESH,
            ).start()
            return carry

        lax.fori_loop(1, 8, send, 0)

    def arrived(step):
        pltpu.make_async_copy(
            mid_buf.at[step, :, pl.ds(0, 4), :], prof_buf.at[step, z], l2.at[step]
        ).wait()
        many(prof_buf.at[step, pl.ds(0, 7)], r2.at[step]).wait()

    for load in loads[0:2] + loads[5:]:
        load.wait()
    lines = pack(3)
    pl.semaphore_wait(barrier, greeted)
    first_leg(3)
    for step in (2, 1, 0):
        lines = lines + pack(step)
        first_leg(step)
    col_send[...] = jnp.broadcast_to(lines[:, None, :], (16, 8, LEV))
    col_mid[pl.ds(q, 1)] = col_send[pl.ds(q, 1)]

    def send_columns(i, carry):
        x2, y2 = xy_peer(i)
        pltpu.make_async_remote_copy(
            col_send.at[x2 * 4 + y2],
            col_mid.at[q],
            col_sem.at[0],
            col_sem.at[1],
            device_id=at_chip(x2, y2, z),
            device_id_type=MESH,
        ).start()
        return carry

    lax.fori_loop(1, 16, send_columns, 0)
    second_leg(3)

    many(grid_in, out_sem).wait()

    def turn(i, carry):
        for u in range(4):
            r = i * 4 + u
            ext[3, r + 1, 8:136, :] = grid_in[r].T
        return carry

    lax.fori_loop(0, ROWS // 4, turn, 0)

    many(col_mid.at[pl.ds(0, 15)], col_sem.at[1]).wait()
    col_line[...] = col_mid[:, 0, :]
    col_recv[pl.ds(z, 1)] = col_line[...][None]

    def send_lines(i, carry):
        z2 = lax.rem(z + i, 8)
        pltpu.make_async_remote_copy(
            col_line,
            col_recv.at[z],
            col_sem.at[2],
            col_sem.at[3],
            device_id=at_chip(x, y, z2),
            device_id_type=MESH,
        ).start()
        return carry

    lax.fori_loop(1, 8, send_lines, 0)
    second_leg(2)

    is_ocean = comp == 0

    def spread_mask(i, carry):
        for u in range(4):
            r = i * 4 + u
            line = jnp.where(is_ocean, mask_ref[pl.ds(r, 1), :].astype(F32), 1.0)
            mask_full[r] = jnp.broadcast_to(line, (COLS, COLS)).T
        return carry

    lax.fori_loop(0, ROWS // 4, spread_mask, 0)

    many(col_recv.at[pl.ds(0, 7)], col_sem.at[3]).wait()
    came = col_recv[...].reshape(128, 128)
    came_row = jnp.floor(came * (1.0 / 128.0))
    came_col = came - came_row * 128.0
    source = lax.broadcasted_iota(I32, (128, SLOTS), 0)
    repeat = jnp.where(source == (lax.broadcasted_iota(I32, (128, SLOTS), 1) >> 2), 1.0, 0.0).astype(BF)
    own_slot = (lax.broadcasted_iota(I32, (16, SLOTS), 0) & 3) == (
        lax.broadcasted_iota(I32, (16, SLOTS), 1) & 3
    )
    for part, value in enumerate((came_row, came_col)):
        col_wide[...] = dot(value.astype(BF), repeat, TN)
        mine = col_wide[pl.ds(pl.multiple_of(z * 16, 16), 16), :]
        mine = jnp.where(own_slot, mine, 0.0)
        for step in range(STEPS):
            col_rows[part, step : step + 1, :] = jnp.sum(
                mine[step * 4 : step * 4 + 4], axis=0, keepdims=True
            )

    def chunk_rows(i):
        return pl.ds(1 + i * HALF, HALF)

    cell = lax.broadcasted_iota(I32, (COLS, SLOTS), 0).astype(F32).astype(BF)

    def match(first, value, second, count):
        wanted = jnp.where(first == value, second, -1.0)
        wanted = jnp.broadcast_to(wanted, (16, SLOTS)).astype(BF)
        wanted = jnp.concatenate([wanted] * (count // 16), axis=0)
        return jnp.where(wanted == cell[0:count], BF(1), BF(0))

    def ids(step):
        return col_rows[0, step : step + 1, :], col_rows[1, step : step + 1, :]

    def row_edges(step):
        high, low = halves(prof_buf[step].reshape(SLOTS, LEV))
        prof_hl[:, 0:LEV] = high
        prof_hl[:, LEV:] = low
        rows_id, cols_id = ids(step)
        onehot[0:128, :] = match(rows_id, 0.0, cols_id, COLS)
        onehot[128:256, :] = match(rows_id, float(ROWS - 1), cols_id, COLS)
        added = dot(onehot[0:256, :], prof_hl[...], NN)
        added = added[:, 0:LEV] + added[:, LEV:]
        edge_row[step, 0] = ext[step, 1, 8:136, :] + added[0:128]
        edge_row[step, 1] = ext[step, ROWS, 8:136, :] + added[128:256]

    def col_edges(step):
        rows_id, cols_id = ids(step)
        onehot[0:32, :] = match(cols_id, 0.0, rows_id, ROWS)
        onehot[32:64, :] = match(cols_id, float(COLS - 1), rows_id, ROWS)
        added = dot(onehot[0:64, :], prof_hl[...], NN)
        added = added[:, 0:LEV] + added[:, LEV:]
        edge_col[step, 0] = ext[step, 1 : ROWS + 1, 8, :] + added[0:32]
        edge_col[step, 1] = ext[step, 1 : ROWS + 1, 135, :] + added[32:64]

    def scatter(step):
        rows_id, cols_id = ids(step)

        def chunk(i, carry):
            for u in range(HALF):
                r = (i * HALF + u).astype(F32)
                onehot[u * COLS : (u + 1) * COLS, :] = match(rows_id, r, cols_id, COLS)
            added = dot(onehot[...], prof_hl[...], NN)
            added = (added[:, 0:LEV] + added[:, LEV:]).reshape(HALF, COLS, LEV)
            ext[step, chunk_rows(i), 8:136, :] = ext[step, chunk_rows(i), 8:136, :] + added
            return carry

        lax.fori_loop(0, 2, chunk, 0)

    def halo_copy(step, side):
        src, dst = (
            (edge_row.at[step, 0], ext.at[step, ROWS + 1, pl.ds(8, COLS)]),
            (edge_row.at[step, 1], ext.at[step, 0, pl.ds(8, COLS)]),
            (edge_col.at[step, 0], halo_col.at[step, 1]),
            (edge_col.at[step, 1], halo_col.at[step, 0]),
            (edge_flux.at[step, 0], halo_flux.at[step, 1]),
            (edge_flux.at[step, 1], halo_flux.at[step, 0]),
        )[side]
        return pltpu.make_async_remote_copy(
            src,
            dst,
            halo_s.at[step, side],
            halo_r.at[step, side],
            device_id=sides[side % 4][1],
            device_id_type=MESH,
        )

    def halo_start(step, which):
        for side in which:

            @pl.when(sides[side % 4][0])
            def _(side=side):
                halo_copy(step, side).start()

    def halo_wait(step, which):
        for side in which:

            @pl.when(sides[side % 4][0])
            def _(side=side):
                halo_copy(step, side).wait_send()
                halo_copy(step, side ^ 1).wait_recv()

    def place_halos(step):
        ext[step, 1 : ROWS + 1, 7, :] = halo_col[step, 0]
        ext[step, 1 : ROWS + 1, 136, :] = halo_col[step, 1]
        if step < 3:
            value = jnp.concatenate([halo_flux[step, 0], halo_flux[step, 1]], axis=1)
            added = dot(in_parts(value), fin_w[...], TN)
            ext[step, 0, 8:136, :] = ext[step, 0, 8:136, :] + added[0:COLS]
            ext[step, ROWS + 1, 8:136, :] = ext[step, ROWS + 1, 8:136, :] + added[COLS:]

    def stencil(step):
        rate = diff_ref[0:1, :]
        rest = 1.0 - 4.0 * rate

        def rows(i, carry):
            for u in range(4):
                r = i * 4 + u
                here = ext[step, r + 1, 8:136, :]
                beside = (
                    ext[step, r, 8:136, :]
                    + ext[step, r + 2, 8:136, :]
                    + ext[step, r + 1, 7:135, :]
                    + ext[step, r + 1, 9:137, :]
                )
                value = (here * rest + beside * rate) * mask_full[r]
                high, low = halves(value)
                at = pl.ds(pl.multiple_of(r * COLS, COLS), COLS)
                state_hl[at, 0:LEV] = high
                state_hl[at, LEV:] = low
            return carry

        lax.fori_loop(0, ROWS // 4, rows, 0)

    def chunk_cells(i):
        return pl.ds(pl.multiple_of(i * HALF * COLS, HALF * COLS), HALF * COLS)

    def surfaces(step):
        def chunk(i, carry):
            both = dot(surf_w[...], state_hl[chunk_cells(i), :], NT)
            total = both[0:8] + both[8:16]
            for j in range(HALF):
                surf[step, i * HALF + j] = total[:, j * COLS : (j + 1) * COLS]
            return carry

        lax.fori_loop(0, 2, chunk, 0)

    def partner_copy(step):
        return pltpu.make_async_remote_copy(
            surf.at[step],
            partner.at[step],
            part_s.at[step],
            part_r.at[step],
            device_id={"comp": 1 - comp},
            device_id_type=MESH,
        )

    def vertical(step):
        def chunk(i, carry):
            mixed = dot(state_hl[chunk_cells(i), :], weights[...], NN)
            mixed = mixed[:, 0:LEV] + mixed[:, LEV:]
            ext[step, chunk_rows(i), 8:136, :] = mixed.reshape(HALF, COLS, LEV)
            return carry

        lax.fori_loop(0, 2, chunk, 0)

    def couple_block(step, b):
        index = coupler_ref[step, pl.ds(pl.multiple_of(b * 8, 8), 8), :]
        lane, row = index & 127, index >> 7
        sums = [jnp.zeros((8, COLS), F32) for _ in range(FIELDS)]
        for r in range(ROWS):
            hit = row == r
            for f in range(FIELDS):
                line = jnp.broadcast_to(partner[step, r, f : f + 1, :], (8, COLS))
                sums[f] = jnp.where(hit, jnp.take_along_axis(line, lane, axis=1), sums[f])
        for f in range(FIELDS):
            for j in range(8):
                received[b * 8 + j, f : f + 1, :] = sums[f][j : j + 1, :]

    def couple(step):
        def block(b, carry):
            couple_block(step, b)
            return carry

        lax.fori_loop(0, 4, block, 0)

    def in_parts(value):
        high = value.astype(BF).astype(F32)
        low = value - high
        return jnp.concatenate([high, low, high, low], axis=0).astype(BF)

    def received_parts(first, count):
        return in_parts(jnp.concatenate([received[first + j] for j in range(count)], axis=1))

    def add_fluxes(step):
        def chunk(i, carry):
            added = dot(received_parts(i * HALF, HALF), fin_w[...], TN).reshape(HALF, COLS, LEV)
            ext[step, chunk_rows(i), 8:136, :] = ext[step, chunk_rows(i), 8:136, :] + added
            return carry

        lax.fori_loop(0, 2, chunk, 0)

    def last_vertical():
        def chunk(i, carry):
            mixed = dot(weights_t[...], state_hl[chunk_cells(i), :], NT)
            mixed = mixed[0:LEV] + mixed[LEV:]
            for j in range(HALF):
                grid_in[i * HALF + j] = mixed[:, j * COLS : (j + 1) * COLS]
            return carry

        lax.fori_loop(0, 2, chunk, 0)

    def last_fluxes():
        def block(b, carry):
            couple_block(0, b)
            added = dot(fin_wt[:, 0:32], received_parts(b * 8, 8), NN)
            for j in range(8):
                r = b * 8 + j
                grid_in[r] = grid_in[r] + added[:, j * COLS : (j + 1) * COLS]
                pltpu.make_async_copy(grid_in.at[r], out_hbm.at[:, r, :], out_sem).start()
            return carry

        lax.fori_loop(0, 4, block, 0)

    for step in (3, 2, 1, 0):
        if step < 3:
            vertical(step)
        arrived(step)
        row_edges(step)
        halo_start(step, (0, 1))
        if step > 1:
            second_leg(step - 2)
        if step < 3:
            partner_copy(step + 1).wait()
            couple(step + 1)
            edge_flux[step, 0] = received[0]
            edge_flux[step, 1] = received[ROWS - 1]
            halo_start(step, (4, 5))
            add_fluxes(step)
        col_edges(step)
        halo_start(step, (2, 3))
        scatter(step)
        halo_wait(step, (0, 1, 2, 3) if step == 3 else (0, 1, 2, 3, 4, 5))
        place_halos(step)
        stencil(step)
        surfaces(step)
        partner_copy(step).start()
    last_vertical()
    partner_copy(0).wait()
    last_fluxes()

    many(col_mid.at[pl.ds(0, 15)], col_sem.at[0]).wait()
    many(col_recv.at[pl.ds(0, 7)], col_sem.at[2]).wait()
    for step in range(STEPS):
        many(mid_buf.at[step, pl.ds(0, 15)], s1.at[step]).wait()
        many(prof_buf.at[step, pl.ds(0, 7)], s2.at[step]).wait()
    many(grid_in, out_sem).wait()


def body(
    final_adjoint,
    innovations,
    obs_owner,
    obs_column,
    coupler,
    sea_mask,
    diffusion,
    vertical,
    flux_out,
    flux_in,
):
    whole = pl.BlockSpec(memory_space=pltpu.HBM)
    dma = pltpu.SemaphoreType.DMA
    result = pl.pallas_call(
        kernel,
        out_shape=jax.ShapeDtypeStruct((LEV, ROWS, COLS), F32),
        in_specs=[whole] * 10,
        out_specs=whole,
        scratch_shapes=[
            pltpu.VMEM((STEPS, 1, PROF), I32),
            pltpu.VMEM((STEPS, 1, PROF), I32),
            pltpu.VMEM((STEPS, ROWS, COLS), I32),
            pltpu.VMEM((ROWS, COLS), I32),
            pltpu.VMEM((1, LEV), F32),
            pltpu.VMEM((LEV, LEV), F32),
            pltpu.VMEM((FIELDS, 1, LEV), F32),
            pltpu.VMEM((FIELDS, 1, LEV), F32),
            pltpu.VMEM((ROWS, LEV, COLS), F32),
            pltpu.VMEM((STEPS, PROF, LEV), F32),
            pltpu.VMEM((STEPS, ROWS + 2, 144, LEV), F32),
            pltpu.VMEM((STEPS, 16, 32, LEV), F32),
            pltpu.VMEM((STEPS, 16, 32, LEV), F32),
            pltpu.VMEM((STEPS, 8, 16, 4, LEV), F32),
            pltpu.VMEM((ROWS * COLS, 2 * LEV), BF),
            pltpu.VMEM((ROWS, COLS, LEV), F32),
            pltpu.VMEM((HALF * COLS, SLOTS), BF),
            pltpu.VMEM((SLOTS, 2 * LEV), BF),
            pltpu.VMEM((16, 8, LEV), F32),
            pltpu.VMEM((16, 8, LEV), F32),
            pltpu.VMEM((16, LEV), F32),
            pltpu.VMEM((8, 16, LEV), F32),
            pltpu.VMEM((128, SLOTS), F32),
            pltpu.VMEM((2, STEPS, SLOTS), F32),
            pltpu.VMEM((STEPS, ROWS, 8, COLS), F32),
            pltpu.VMEM((STEPS, ROWS, 8, COLS), F32),
            pltpu.VMEM((ROWS, 8, COLS), F32),
            pltpu.VMEM((256, 256), BF),
            pltpu.VMEM((256, 256), BF),
            pltpu.VMEM((16, 256), BF),
            pltpu.VMEM((32, LEV), BF),
            pltpu.VMEM((LEV, 128), BF),
            pltpu.VMEM((16, LEV), F32),
            pltpu.VMEM((STEPS, 2, COLS, LEV), F32),
            pltpu.VMEM((STEPS, 2, ROWS, LEV), F32),
            pltpu.VMEM((STEPS, 2, ROWS, LEV), F32),
            pltpu.VMEM((STEPS, 2, 8, COLS), F32),
            pltpu.VMEM((STEPS, 2, 8, COLS), F32),
            dma((9,)),
            dma((STEPS,)),
            dma((STEPS,)),
            dma((STEPS,)),
            dma((STEPS,)),
            dma((STEPS,)),
            dma((STEPS,)),
            dma((4,)),
            dma((STEPS, 6)),
            dma((STEPS, 6)),
            dma((STEPS,)),
            dma((STEPS,)),
            dma,
        ],
        compiler_params=pltpu.CompilerParams(
            collective_id=0, has_side_effects=True, vmem_limit_bytes=64 * 2**20
        ),
    )(
        final_adjoint.reshape(LEV, ROWS, COLS),
        innovations.reshape(STEPS, PROF, LEV),
        obs_owner.reshape(STEPS, 1, PROF),
        obs_column.reshape(STEPS, 1, PROF),
        coupler.reshape(STEPS, ROWS, COLS),
        sea_mask,
        diffusion,
        vertical[0],
        flux_out.reshape(FIELDS, 1, LEV),
        flux_in[0].T.reshape(FIELDS, 1, LEV),
    )
    return result.reshape(1, LEV, ROWS, COLS)


def solution(mesh):
    placed = (
        P("comp", None, "gx", "gy"),
        P(None, "comp", ("gx", "gy"), None),
        P(None, "comp", ("gx", "gy"), None),
        P(None, "comp", ("gx", "gy")),
        P(None, "comp", "gx", "gy"),
        P("gx", "gy"),
        P("comp", None),
        P("comp", None, None),
        P("comp", None, None),
        P("comp", None, None),
    )
    return jax.shard_map(
        body, mesh=mesh, in_specs=placed, out_specs=P("comp", None, "gx", "gy"), check_vma=False
    )
```

```python
import jax
import jax.numpy as jnp
from jax import lax
from jax.experimental import pallas as pl
from jax.experimental.pallas import tpu as pltpu
from jax.sharding import PartitionSpec as P

MESH = pl.DeviceIdType.MESH
STEPS = 4
ROWS = 32
COLS = 128
LEV = 128
PROF = 256
SLOTS = 512
FIELDS = 5
HALF = ROWS // 2
BF = jnp.bfloat16
F32 = jnp.float32
I32 = jnp.int32

NN = (((1,), (0,)), ((), ()))
NT = (((1,), (1,)), ((), ()))
TN = (((0,), (0,)), ((), ()))


def dot(a, b, dims):
    return lax.dot_general(a, b, dims, preferred_element_type=F32)


def halves(value):
    high = value.astype(BF)
    low = (value - high.astype(F32)).astype(BF)
    return high, low


def at_chip(x, y, z):
    return {"gx": x * 4 + z // 2, "gy": lax.rem(z, 2) * 4 + y}


def kernel(
    state_hbm,
    innov_hbm,
    owner_hbm,
    column_hbm,
    coupler_hbm,
    mask_hbm,
    diff_hbm,
    vert_hbm,
    fout_hbm,
    fin_hbm,
    out_hbm,
    owner_ref,
    column_ref,
    coupler_ref,
    mask_ref,
    diff_ref,
    vert_ref,
    fout_ref,
    fin_ref,
    grid_in,
    innov,
    ext,
    send_buf,
    mid_buf,
    prof_buf,
    state_hl,
    mask_full,
    onehot,
    prof_hl,
    col_send,
    col_mid,
    col_line,
    col_recv,
    col_wide,
    col_rows,
    surf,
    partner,
    received,
    weights,
    weights_t,
    surf_w,
    fin_w,
    fin_wt,
    small,
    edge_row,
    edge_col,
    halo_col,
    edge_flux,
    halo_flux,
    load_sem,
    s1,
    r1,
    l1,
    s2,
    r2,
    l2,
    col_sem,
    halo_s,
    halo_r,
    part_s,
    part_r,
    out_sem,
):
    comp = lax.axis_index("comp")
    gx = lax.axis_index("gx")
    gy = lax.axis_index("gy")
    x, y = gx // 4, lax.rem(gy, 4)
    z = lax.rem(gx, 4) * 2 + gy // 4
    q = x * 4 + y

    loads = [
        pltpu.make_async_copy(src, dst, load_sem.at[i])
        for i, (src, dst) in enumerate(
            (
                (owner_hbm, owner_ref),
                (innov_hbm, innov),
                (vert_hbm, vert_ref),
                (fout_hbm, fout_ref),
                (fin_hbm, fin_ref),
                (column_hbm, column_ref),
                (coupler_hbm, coupler_ref),
                (mask_hbm, mask_ref),
                (diff_hbm, diff_ref),
            )
        )
    ]
    for load in loads:
        load.start()

    def load_row(r, carry):
        pltpu.make_async_copy(state_hbm.at[:, r, :], grid_in.at[r], out_sem).start()
        return carry

    lax.fori_loop(0, ROWS, load_row, 0)

    def zero_edges(step, carry):
        ext[step, 0] = jnp.zeros((144, LEV), F32)
        ext[step, ROWS + 1] = jnp.zeros((144, LEV), F32)
        halo_col[step] = jnp.zeros((2, ROWS, LEV), F32)
        halo_flux[step] = jnp.zeros((2, 8, COLS), F32)
        return carry

    lax.fori_loop(0, STEPS, zero_edges, 0)

    def xy_peer(i):
        return lax.rem(x + i // 4, 4), lax.rem(y + lax.rem(i, 4), 4)

    barrier = pltpu.get_barrier_semaphore()

    def greet(target):
        pl.semaphore_signal(barrier, inc=1, device_id=target, device_id_type=MESH)

    for i in range(1, 16):
        x2, y2 = xy_peer(jnp.int32(i))
        greet(at_chip(x2, y2, z))
    for i in range(1, 8):
        greet(at_chip(x, y, lax.rem(z + i, 8)))
    greet({"comp": 1 - comp})

    sides = (
        (gx > 0, {"gx": gx - 1}),
        (gx < 15, {"gx": gx + 1}),
        (gy > 0, {"gy": gy - 1}),
        (gy < 7, {"gy": gy + 1}),
    )
    for there, target in sides:

        @pl.when(there)
        def _(target=target):
            greet(target)

    greeted = 23
    for there, _ in sides:
        greeted = greeted + jnp.where(there, 1, 0)

    for load in loads[2:5]:
        load.wait()
    vert = vert_ref[...]
    v_high, v_low = halves(vert)
    weights[0:128, 0:128] = v_high
    weights[128:256, 0:128] = v_high
    weights[0:128, 128:256] = v_low
    weights[128:256, 128:256] = v_low
    vt_high, vt_low = halves(vert.T)
    weights_t[0:128, 0:128] = vt_high
    weights_t[0:128, 128:256] = vt_high
    weights_t[128:256, 0:128] = vt_low
    weights_t[128:256, 128:256] = vt_low
    small[...] = jnp.zeros((16, LEV), F32)
    for f in range(FIELDS):
        small[f : f + 1, :] = fout_ref[f]
        small[8 + f : 9 + f, :] = fin_ref[f]
    flux_w = lax.dot_general(
        small[0:8, :], vert, NT, precision=lax.Precision.HIGHEST, preferred_element_type=F32
    )
    g_high = flux_w.astype(BF).astype(F32)
    g_both = jnp.concatenate([g_high, flux_w - g_high], axis=0).astype(BF)
    surf_w[:, 0:128] = g_both
    surf_w[:, 128:256] = g_both
    fin = small[8:16, :]
    f_high = fin.astype(BF).astype(F32)
    f_all = jnp.concatenate([f_high, f_high, fin - f_high, jnp.zeros((8, LEV), F32)], axis=0)
    fin_w[...] = f_all.astype(BF)
    f_pad = jnp.concatenate([f_all, jnp.zeros((96, LEV), F32)], axis=0)
    fin_wt[...] = f_pad.T.astype(BF)
    received[...] = jnp.zeros((ROWS, 8, COLS), F32)

    lane_b = lax.broadcasted_iota(I32, (128, 128), 1)
    sub_b = lax.broadcasted_iota(I32, (128, 128), 0)
    earlier = sub_b < lane_b

    def slot_of(step):
        owner = owner_ref[step]
        first, second = owner[:, 0:128], owner[:, 128:256]
        first_b = jnp.broadcast_to(first, (128, 128))
        second_b = jnp.broadcast_to(second, (128, 128))
        first_t = first_b.astype(F32).T.astype(I32)
        second_t = second_b.astype(F32).T.astype(I32)
        one = jnp.where((first_t == first_b) & earlier, 1, 0)
        two = jnp.where(first_t == second_b, 1, 0)
        three = jnp.where((second_t == second_b) & earlier, 1, 0)
        rank = jnp.concatenate(
            [
                jnp.sum(one, axis=0, keepdims=True),
                jnp.sum(two + three, axis=0, keepdims=True),
            ],
            axis=1,
        )
        owner_q = (owner >> 5) * 4 + (owner & 3)
        owner_z = ((owner >> 3) & 3) * 2 + ((owner >> 2) & 1)
        return owner_q, owner_z, rank

    def pack(step):
        owner_q, owner_z, rank = slot_of(step)
        slot = (owner_q * 8 + owner_z) * 4 + rank
        placing = jnp.where(
            jnp.broadcast_to(slot, (SLOTS, PROF)) == lax.broadcasted_iota(I32, (SLOTS, PROF), 0),
            1.0,
            0.0,
        ).astype(BF)
        high, low = halves(innov[step])
        placed = dot(placing, jnp.concatenate([high, low], axis=1), NN)
        send_buf[step] = (placed[:, 0:LEV] + placed[:, LEV:]).reshape(16, 32, LEV)
        columns = column_ref[step]
        to_q = jnp.broadcast_to(owner_q, (16, PROF)) == lax.broadcasted_iota(I32, (16, PROF), 0)
        row_part = jnp.where(to_q, (columns >> 7).astype(F32), 0.0)
        col_part = jnp.where(to_q, (columns & 127).astype(F32), 0.0)
        both = jnp.concatenate([row_part, col_part], axis=0).astype(BF)
        lane = owner_z * 16 + step * 4 + rank
        spread = jnp.where(
            jnp.broadcast_to(lane, (128, PROF)) == lax.broadcasted_iota(I32, (128, PROF), 0),
            1.0,
            0.0,
        ).astype(BF)
        lines = dot(both, spread, NT)
        return lines[0:16] * 128.0 + lines[16:32]

    def first_leg(step):
        pltpu.make_async_copy(send_buf.at[step, q], mid_buf.at[step, q], l1.at[step]).start()

        def send(i, carry):
            x2, y2 = xy_peer(i)
            pltpu.make_async_remote_copy(
                send_buf.at[step, x2 * 4 + y2],
                mid_buf.at[step, q],
                s1.at[step],
                r1.at[step],
                device_id=at_chip(x2, y2, z),
                device_id_type=MESH,
            ).start()
            return carry

        lax.fori_loop(1, 16, send, 0)

    def many(ref, sem):
        return pltpu.make_async_copy(ref, ref, sem)

    def second_leg(step):
        pltpu.make_async_copy(send_buf.at[step, q], mid_buf.at[step, q], l1.at[step]).wait()
        many(mid_buf.at[step, pl.ds(0, 15)], r1.at[step]).wait()

        def block(z2):
            return mid_buf.at[step, :, pl.ds(pl.multiple_of(z2 * 4, 4), 4), :]

        pltpu.make_async_copy(block(z), prof_buf.at[step, z], l2.at[step]).start()

        def send(i, carry):
            z2 = lax.rem(z + i, 8)
            pltpu.make_async_remote_copy(
                block(z2),
                prof_buf.at[step, z],
                s2.at[step],
                r2.at[step],
                device_id=at_chip(x, y, z2),
                device_id_type=MESH,
            ).start()
            return carry

        lax.fori_loop(1, 8, send, 0)

    def arrived(step):
        pltpu.make_async_copy(
            mid_buf.at[step, :, pl.ds(0, 4), :], prof_buf.at[step, z], l2.at[step]
        ).wait()
        many(prof_buf.at[step, pl.ds(0, 7)], r2.at[step]).wait()

    for load in loads[0:2] + loads[5:]:
        load.wait()
    lines = pack(3)
    pl.semaphore_wait(barrier, greeted)
    first_leg(3)
    for step in (2, 1, 0):
        lines = lines + pack(step)
    col_send[...] = jnp.broadcast_to(lines[:, None, :], (16, 8, LEV))
    col_mid[pl.ds(q, 1)] = col_send[pl.ds(q, 1)]

    def send_columns(i, carry):
        x2, y2 = xy_peer(i)
        pltpu.make_async_remote_copy(
            col_send.at[x2 * 4 + y2],
            col_mid.at[q],
            col_sem.at[0],
            col_sem.at[1],
            device_id=at_chip(x2, y2, z),
            device_id_type=MESH,
        ).start()
        return carry

    lax.fori_loop(1, 16, send_columns, 0)
    second_leg(3)
    first_leg(2)

    many(grid_in, out_sem).wait()

    def turn(i, carry):
        for u in range(4):
            r = i * 4 + u
            ext[3, r + 1, 8:136, :] = grid_in[r].T
        return carry

    lax.fori_loop(0, ROWS // 4, turn, 0)

    many(col_mid.at[pl.ds(0, 15)], col_sem.at[1]).wait()
    col_line[...] = col_mid[:, 0, :]
    col_recv[pl.ds(z, 1)] = col_line[...][None]

    def send_lines(i, carry):
        z2 = lax.rem(z + i, 8)
        pltpu.make_async_remote_copy(
            col_line,
            col_recv.at[z],
            col_sem.at[2],
            col_sem.at[3],
            device_id=at_chip(x, y, z2),
            device_id_type=MESH,
        ).start()
        return carry

    lax.fori_loop(1, 8, send_lines, 0)
    second_leg(2)
    first_leg(1)

    is_ocean = comp == 0

    def spread_mask(i, carry):
        for u in range(4):
            r = i * 4 + u
            line = jnp.where(is_ocean, mask_ref[pl.ds(r, 1), :].astype(F32), 1.0)
            mask_full[r] = jnp.broadcast_to(line, (COLS, COLS)).T
        return carry

    lax.fori_loop(0, ROWS // 4, spread_mask, 0)

    many(col_recv.at[pl.ds(0, 7)], col_sem.at[3]).wait()
    came = col_recv[...].reshape(128, 128)
    came_row = jnp.floor(came * (1.0 / 128.0))
    came_col = came - came_row * 128.0
    source = lax.broadcasted_iota(I32, (128, SLOTS), 0)
    repeat = jnp.where(source == (lax.broadcasted_iota(I32, (128, SLOTS), 1) >> 2), 1.0, 0.0).astype(BF)
    own_slot = (lax.broadcasted_iota(I32, (16, SLOTS), 0) & 3) == (
        lax.broadcasted_iota(I32, (16, SLOTS), 1) & 3
    )
    for part, value in enumerate((came_row, came_col)):
        col_wide[...] = dot(value.astype(BF), repeat, TN)
        mine = col_wide[pl.ds(pl.multiple_of(z * 16, 16), 16), :]
        mine = jnp.where(own_slot, mine, 0.0)
        for step in range(STEPS):
            col_rows[part, step : step + 1, :] = jnp.sum(
                mine[step * 4 : step * 4 + 4], axis=0, keepdims=True
            )

    def chunk_rows(i):
        return pl.ds(1 + i * HALF, HALF)

    cell = lax.broadcasted_iota(I32, (COLS, SLOTS), 0).astype(F32).astype(BF)

    def match(first, value, second, count):
        wanted = jnp.where(first == value, second, -1.0)
        wanted = jnp.broadcast_to(wanted, (16, SLOTS)).astype(BF)
        wanted = jnp.concatenate([wanted] * (count // 16), axis=0)
        return jnp.where(wanted == cell[0:count], BF(1), BF(0))

    def ids(step):
        return col_rows[0, step : step + 1, :], col_rows[1, step : step + 1, :]

    def row_edges(step):
        high, low = halves(prof_buf[step].reshape(SLOTS, LEV))
        prof_hl[:, 0:LEV] = high
        prof_hl[:, LEV:] = low
        rows_id, cols_id = ids(step)
        onehot[0:128, :] = match(rows_id, 0.0, cols_id, COLS)
        onehot[128:256, :] = match(rows_id, float(ROWS - 1), cols_id, COLS)
        added = dot(onehot[0:256, :], prof_hl[...], NN)
        added = added[:, 0:LEV] + added[:, LEV:]
        edge_row[step, 0] = ext[step, 1, 8:136, :] + added[0:128]
        edge_row[step, 1] = ext[step, ROWS, 8:136, :] + added[128:256]

    def col_edges(step):
        rows_id, cols_id = ids(step)
        onehot[0:32, :] = match(cols_id, 0.0, rows_id, ROWS)
        onehot[32:64, :] = match(cols_id, float(COLS - 1), rows_id, ROWS)
        added = dot(onehot[0:64, :], prof_hl[...], NN)
        added = added[:, 0:LEV] + added[:, LEV:]
        edge_col[step, 0] = ext[step, 1 : ROWS + 1, 8, :] + added[0:32]
        edge_col[step, 1] = ext[step, 1 : ROWS + 1, 135, :] + added[32:64]

    def scatter(step):
        rows_id, cols_id = ids(step)

        def chunk(i, carry):
            for u in range(HALF):
                r = (i * HALF + u).astype(F32)
                onehot[u * COLS : (u + 1) * COLS, :] = match(rows_id, r, cols_id, COLS)
            added = dot(onehot[...], prof_hl[...], NN)
            added = (added[:, 0:LEV] + added[:, LEV:]).reshape(HALF, COLS, LEV)
            ext[step, chunk_rows(i), 8:136, :] = ext[step, chunk_rows(i), 8:136, :] + added
            return carry

        lax.fori_loop(0, 2, chunk, 0)

    def halo_copy(step, side):
        src, dst = (
            (edge_row.at[step, 0], ext.at[step, ROWS + 1, pl.ds(8, COLS)]),
            (edge_row.at[step, 1], ext.at[step, 0, pl.ds(8, COLS)]),
            (edge_col.at[step, 0], halo_col.at[step, 1]),
            (edge_col.at[step, 1], halo_col.at[step, 0]),
            (edge_flux.at[step, 0], halo_flux.at[step, 1]),
            (edge_flux.at[step, 1], halo_flux.at[step, 0]),
        )[side]
        return pltpu.make_async_remote_copy(
            src,
            dst,
            halo_s.at[step, side],
            halo_r.at[step, side],
            device_id=sides[side % 4][1],
            device_id_type=MESH,
        )

    def halo_start(step, which):
        for side in which:

            @pl.when(sides[side % 4][0])
            def _(side=side):
                halo_copy(step, side).start()

    def halo_wait(step, which):
        for side in which:

            @pl.when(sides[side % 4][0])
            def _(side=side):
                halo_copy(step, side).wait_send()
                halo_copy(step, side ^ 1).wait_recv()

    def place_halos(step):
        ext[step, 1 : ROWS + 1, 7, :] = halo_col[step, 0]
        ext[step, 1 : ROWS + 1, 136, :] = halo_col[step, 1]
        if step < 3:
            value = jnp.concatenate([halo_flux[step, 0], halo_flux[step, 1]], axis=1)
            added = dot(in_parts(value), fin_w[...], TN)
            ext[step, 0, 8:136, :] = ext[step, 0, 8:136, :] + added[0:COLS]
            ext[step, ROWS + 1, 8:136, :] = ext[step, ROWS + 1, 8:136, :] + added[COLS:]

    def stencil(step):
        rate = diff_ref[0:1, :]
        rest = 1.0 - 4.0 * rate

        def rows(i, carry):
            for u in range(4):
                r = i * 4 + u
                here = ext[step, r + 1, 8:136, :]
                beside = (
                    ext[step, r, 8:136, :]
                    + ext[step, r + 2, 8:136, :]
                    + ext[step, r + 1, 7:135, :]
                    + ext[step, r + 1, 9:137, :]
                )
                value = (here * rest + beside * rate) * mask_full[r]
                high, low = halves(value)
                at = pl.ds(pl.multiple_of(r * COLS, COLS), COLS)
                state_hl[at, 0:LEV] = high
                state_hl[at, LEV:] = low
            return carry

        lax.fori_loop(0, ROWS // 4, rows, 0)

    def chunk_cells(i):
        return pl.ds(pl.multiple_of(i * HALF * COLS, HALF * COLS), HALF * COLS)

    def surfaces(step):
        def chunk(i, carry):
            both = dot(surf_w[...], state_hl[chunk_cells(i), :], NT)
            total = both[0:8] + both[8:16]
            for j in range(HALF):
                surf[step, i * HALF + j] = total[:, j * COLS : (j + 1) * COLS]
            return carry

        lax.fori_loop(0, 2, chunk, 0)

    def partner_copy(step):
        return pltpu.make_async_remote_copy(
            surf.at[step],
            partner.at[step],
            part_s.at[step],
            part_r.at[step],
            device_id={"comp": 1 - comp},
            device_id_type=MESH,
        )

    def vertical(step):
        def chunk(i, carry):
            mixed = dot(state_hl[chunk_cells(i), :], weights[...], NN)
            mixed = mixed[:, 0:LEV] + mixed[:, LEV:]
            ext[step, chunk_rows(i), 8:136, :] = mixed.reshape(HALF, COLS, LEV)
            return carry

        lax.fori_loop(0, 2, chunk, 0)

    def couple_block(step, b):
        index = coupler_ref[step, pl.ds(pl.multiple_of(b * 8, 8), 8), :]
        lane, row = index & 127, index >> 7
        sums = [jnp.zeros((8, COLS), F32) for _ in range(FIELDS)]
        for r in range(ROWS):
            hit = row == r
            for f in range(FIELDS):
                line = jnp.broadcast_to(partner[step, r, f : f + 1, :], (8, COLS))
                sums[f] = jnp.where(hit, jnp.take_along_axis(line, lane, axis=1), sums[f])
        for f in range(FIELDS):
            for j in range(8):
                received[b * 8 + j, f : f + 1, :] = sums[f][j : j + 1, :]

    def couple(step):
        def block(b, carry):
            couple_block(step, b)
            return carry

        lax.fori_loop(0, 4, block, 0)

    def in_parts(value):
        high = value.astype(BF).astype(F32)
        low = value - high
        return jnp.concatenate([high, low, high, low], axis=0).astype(BF)

    def received_parts(first, count):
        return in_parts(jnp.concatenate([received[first + j] for j in range(count)], axis=1))

    def add_fluxes(step):
        def chunk(i, carry):
            added = dot(received_parts(i * HALF, HALF), fin_w[...], TN).reshape(HALF, COLS, LEV)
            ext[step, chunk_rows(i), 8:136, :] = ext[step, chunk_rows(i), 8:136, :] + added
            return carry

        lax.fori_loop(0, 2, chunk, 0)

    def last_vertical():
        def chunk(i, carry):
            mixed = dot(weights_t[...], state_hl[chunk_cells(i), :], NT)
            mixed = mixed[0:LEV] + mixed[LEV:]
            for j in range(HALF):
                grid_in[i * HALF + j] = mixed[:, j * COLS : (j + 1) * COLS]
            return carry

        lax.fori_loop(0, 2, chunk, 0)

    def last_fluxes():
        def block(b, carry):
            couple_block(0, b)
            added = dot(fin_wt[:, 0:32], received_parts(b * 8, 8), NN)
            for j in range(8):
                r = b * 8 + j
                grid_in[r] = grid_in[r] + added[:, j * COLS : (j + 1) * COLS]
                pltpu.make_async_copy(grid_in.at[r], out_hbm.at[:, r, :], out_sem).start()
            return carry

        lax.fori_loop(0, 4, block, 0)

    for step in (3, 2, 1, 0):
        if step < 3:
            vertical(step)
        arrived(step)
        row_edges(step)
        halo_start(step, (0, 1))
        if step < 3:
            partner_copy(step + 1).wait()
            couple(step + 1)
            edge_flux[step, 0] = received[0]
            edge_flux[step, 1] = received[ROWS - 1]
            halo_start(step, (4, 5))
            add_fluxes(step)
        col_edges(step)
        halo_start(step, (2, 3))
        if step > 1:
            second_leg(step - 2)
            if step == 3:
                first_leg(0)
        scatter(step)
        halo_wait(step, (0, 1, 2, 3) if step == 3 else (0, 1, 2, 3, 4, 5))
        place_halos(step)
        stencil(step)
        surfaces(step)
        partner_copy(step).start()
    last_vertical()
    partner_copy(0).wait()
    last_fluxes()

    many(col_mid.at[pl.ds(0, 15)], col_sem.at[0]).wait()
    many(col_recv.at[pl.ds(0, 7)], col_sem.at[2]).wait()
    for step in range(STEPS):
        many(mid_buf.at[step, pl.ds(0, 15)], s1.at[step]).wait()
        many(prof_buf.at[step, pl.ds(0, 7)], s2.at[step]).wait()
    many(grid_in, out_sem).wait()


def body(
    final_adjoint,
    innovations,
    obs_owner,
    obs_column,
    coupler,
    sea_mask,
    diffusion,
    vertical,
    flux_out,
    flux_in,
):
    whole = pl.BlockSpec(memory_space=pltpu.HBM)
    dma = pltpu.SemaphoreType.DMA
    result = pl.pallas_call(
        kernel,
        out_shape=jax.ShapeDtypeStruct((LEV, ROWS, COLS), F32),
        in_specs=[whole] * 10,
        out_specs=whole,
        scratch_shapes=[
            pltpu.VMEM((STEPS, 1, PROF), I32),
            pltpu.VMEM((STEPS, 1, PROF), I32),
            pltpu.VMEM((STEPS, ROWS, COLS), I32),
            pltpu.VMEM((ROWS, COLS), I32),
            pltpu.VMEM((1, LEV), F32),
            pltpu.VMEM((LEV, LEV), F32),
            pltpu.VMEM((FIELDS, 1, LEV), F32),
            pltpu.VMEM((FIELDS, 1, LEV), F32),
            pltpu.VMEM((ROWS, LEV, COLS), F32),
            pltpu.VMEM((STEPS, PROF, LEV), F32),
            pltpu.VMEM((STEPS, ROWS + 2, 144, LEV), F32),
            pltpu.VMEM((STEPS, 16, 32, LEV), F32),
            pltpu.VMEM((STEPS, 16, 32, LEV), F32),
            pltpu.VMEM((STEPS, 8, 16, 4, LEV), F32),
            pltpu.VMEM((ROWS * COLS, 2 * LEV), BF),
            pltpu.VMEM((ROWS, COLS, LEV), F32),
            pltpu.VMEM((HALF * COLS, SLOTS), BF),
            pltpu.VMEM((SLOTS, 2 * LEV), BF),
            pltpu.VMEM((16, 8, LEV), F32),
            pltpu.VMEM((16, 8, LEV), F32),
            pltpu.VMEM((16, LEV), F32),
            pltpu.VMEM((8, 16, LEV), F32),
            pltpu.VMEM((128, SLOTS), F32),
            pltpu.VMEM((2, STEPS, SLOTS), F32),
            pltpu.VMEM((STEPS, ROWS, 8, COLS), F32),
            pltpu.VMEM((STEPS, ROWS, 8, COLS), F32),
            pltpu.VMEM((ROWS, 8, COLS), F32),
            pltpu.VMEM((256, 256), BF),
            pltpu.VMEM((256, 256), BF),
            pltpu.VMEM((16, 256), BF),
            pltpu.VMEM((32, LEV), BF),
            pltpu.VMEM((LEV, 128), BF),
            pltpu.VMEM((16, LEV), F32),
            pltpu.VMEM((STEPS, 2, COLS, LEV), F32),
            pltpu.VMEM((STEPS, 2, ROWS, LEV), F32),
            pltpu.VMEM((STEPS, 2, ROWS, LEV), F32),
            pltpu.VMEM((STEPS, 2, 8, COLS), F32),
            pltpu.VMEM((STEPS, 2, 8, COLS), F32),
            dma((9,)),
            dma((STEPS,)),
            dma((STEPS,)),
            dma((STEPS,)),
            dma((STEPS,)),
            dma((STEPS,)),
            dma((STEPS,)),
            dma((4,)),
            dma((STEPS, 6)),
            dma((STEPS, 6)),
            dma((STEPS,)),
            dma((STEPS,)),
            dma,
        ],
        compiler_params=pltpu.CompilerParams(
            collective_id=0, has_side_effects=True, vmem_limit_bytes=64 * 2**20
        ),
    )(
        final_adjoint.reshape(LEV, ROWS, COLS),
        innovations.reshape(STEPS, PROF, LEV),
        obs_owner.reshape(STEPS, 1, PROF),
        obs_column.reshape(STEPS, 1, PROF),
        coupler.reshape(STEPS, ROWS, COLS),
        sea_mask,
        diffusion,
        vertical[0],
        flux_out.reshape(FIELDS, 1, LEV),
        flux_in[0].T.reshape(FIELDS, 1, LEV),
    )
    return result.reshape(1, LEV, ROWS, COLS)


def solution(mesh):
    placed = (
        P("comp", None, "gx", "gy"),
        P(None, "comp", ("gx", "gy"), None),
        P(None, "comp", ("gx", "gy"), None),
        P(None, "comp", ("gx", "gy")),
        P(None, "comp", "gx", "gy"),
        P("gx", "gy"),
        P("comp", None),
        P("comp", None, None),
        P("comp", None, None),
        P("comp", None, None),
    )
    return jax.shard_map(
        body, mesh=mesh, in_specs=placed, out_specs=P("comp", None, "gx", "gy"), check_vma=False
    )
```
